512 devices in a mesh: branch: 2 (over core), dp: 128 (over z_hi, x, y), seq: 2 (over z_lo).
Axes of the slice: x: 4, y: 8, z: 8 (z_hi: 4, z_lo: 2; z = z_hi * 2 + z_lo), core: 2. Of those that a mesh axis runs over, the one named last changes fastest.
Arguments:
- attn: bfloat16 [2, 32768, 2432], P('branch', ('dp', 'seq')), may hold values from -24 to 24
- hidden: bfloat16 [2, 32768, 2432], P('branch', ('dp', 'seq')), may hold values from -6 to 6
- noisy: bfloat16 [32768, 2432], P(('dp', 'seq')), may hold values from -6 to 6
- target: bfloat16 [32768, 2432], P(('dp', 'seq')), may hold values from -6 to 6
- quantized_weight_codes: bfloat16 [2432, 2432], P('dp'), may hold values from -0.0625 to 0.0625
- weight_exponents: int32 [2432, 19], P('dp'), may hold values from -1 to 2
- adapter_down_map: bfloat16 [2432, 128], replicated, may hold values from -0.125 to 0.125
- adapter_up_transposed: bfloat16 [2432, 128], replicated, may hold values from -0.5 to 0.5
- gates: float32 [2, 8, 2432], P('branch'), may hold values from 0.25 to 1.5
- group_prompt: int32 [128], P('dp'), may hold values from 0 to 7
- step_index: int32 [1], replicated, may hold values from 14 to 28
Outputs:
- grad_attn: bfloat16 [2, 32768, 2432], P('branch', ('dp', 'seq'))
- grad_down: float32 [2432, 128], P('dp')
- grad_up_t: float32 [2432, 128], P('dp')
The draws below stay inside these ranges and needn't reach their ends.
All inputs are finite; a program needn't handle non-finite values.
Results may differ from the reference program's by a relative error of at most 0.01.
Values may be sent and summed in bfloat16 or wider, within the bound.
No kernel may reach another device: no remote copies, remote signals or barrier semaphores. Data moves between devices by JAX's collectives and lax.ppermute only.
A program may use at most 128 MiB of HBM per device.

```python
import jax
import jax.numpy as jnp
from jax import lax

MODEL_WIDTH = 2432
ADAPTER_RANK = 128
QBLOCK = 128
PROMPTS = 8
STEPS = 28
TOK_DEV = 128
TOKENS = 32768
GROUPS = 128
N_SEQ = 2


def with_ends(entries, rng, least, top_value):
    spot = [jax.random.randint(jax.random.fold_in(rng, axis), (), 0, length) for axis, length in enumerate(entries.shape)]
    widest = entries.shape.index(max(entries.shape))
    neighbour = spot[:widest] + [(spot[widest] + 1) % entries.shape[widest]] + spot[widest + 1:]
    return entries.at[tuple(spot)].set(least).at[tuple(neighbour)].set(top_value)


def strengthened(drawn, own_key, source, target, parts, factor):
    def block_of(dim):
        return (jnp.arange(drawn.shape[dim]) // (drawn.shape[dim] // parts)).reshape((-1,) + (1,) * (drawn.ndim - 1 - dim))

    near = jax.random.permutation(own_key, parts)[block_of(target)]
    second = (block_of(target) + parts // 2) % parts
    return jnp.where((block_of(source) == near) | (block_of(source) == second), factor * drawn, drawn)


def levels(key, shape, split, smallest, top_value):
    factor_of, own = 1.0, jax.random.fold_in(key, 6)
    for axis_at, blocks in split:
        draws = jnp.exp(jax.random.uniform(jax.random.fold_in(own, axis_at), (blocks,), jnp.float32, smallest / len(split), top_value / len(split)))
        factor_of = factor_of * jnp.repeat(draws, shape[axis_at] // blocks).reshape([-1 if axis == axis_at else 1 for axis in range(len(shape))])
    return factor_of


def centred(rng, dims, width, limit, cuts=(), held_as=jnp.bfloat16):
    array = width * jax.random.normal(rng, dims, jnp.float32)
    if cuts:
        array = array * levels(rng, dims, cuts, -0.22, 0.18)
    return jnp.clip(array, -limit, limit).astype(held_as)


def bell_draw_with(key, extent, scale, limit, pieces, heavy, kind=jnp.bfloat16):
    values = scale * jax.random.normal(key, extent, jnp.float32)
    if pieces:
        values = values * levels(key, extent, pieces, -0.22, 0.18)
    return jnp.clip(strengthened(values, jax.random.fold_in(key, 3), *heavy), -limit, limit).astype(kind)


def setup_inputs(seed: int = 0) -> dict:
    keys = jax.random.split(jax.random.key(seed), 12)
    return {
        "attn": bell_draw_with(keys[0], (2, TOKENS, MODEL_WIDTH), 1.0, 24.0, ((0, 2), (1, 256)), (1, 2, 128, 5.5)),
        "hidden": centred(keys[1], (2, TOKENS, MODEL_WIDTH), 1.0, 6.0, ((0, 2), (1, 256))),
        "noisy": centred(keys[2], (TOKENS, MODEL_WIDTH), 1.0, 6.0, ((0, 256),)),
        "target": centred(keys[3], (TOKENS, MODEL_WIDTH), 1.0, 6.0, ((0, 256),)),
        "quantized_weight_codes": centred(keys[4], (MODEL_WIDTH, MODEL_WIDTH), (4 * MODEL_WIDTH) ** -0.5, 0.0625, ((0, 128),)),
        "weight_exponents": with_ends(jax.random.randint(keys[5], (MODEL_WIDTH, MODEL_WIDTH // QBLOCK), -1, 3), jax.random.fold_in(keys[5], 1), -1, 2).astype(jnp.int32),
        "adapter_down_map": centred(keys[6], (MODEL_WIDTH, ADAPTER_RANK), MODEL_WIDTH ** -0.5, 0.125),
        "adapter_up_transposed": centred(keys[7], (MODEL_WIDTH, ADAPTER_RANK), ADAPTER_RANK ** -0.5, 0.5),
        "gates": jnp.clip(0.25 + 1.25 * jax.random.uniform(keys[8], (2, PROMPTS, MODEL_WIDTH), jnp.float32) ** levels(keys[8], (2, PROMPTS, MODEL_WIDTH), ((0, 2),), -0.2, 0.2), 0.25, 1.5),
        "group_prompt": with_ends(jax.random.randint(keys[9], (GROUPS,), 0, PROMPTS), jax.random.fold_in(keys[9], 1), 0, PROMPTS - 1).astype(jnp.int32),
        "step_index": jax.random.randint(keys[10], (1,), STEPS // 2, STEPS + 1).astype(jnp.int32),
    }


GUIDE = 4.5
REWARD = 0.08
ADAPTER_STRENGTH = 0.5
SHIFT = 3.0


def noise_level(step_index):
    frac = step_index[0].astype(jnp.float32) / STEPS
    return SHIFT * frac / (1.0 + (SHIFT - 1.0) * frac)


def dequantize(codes, exps):
    count = codes.shape[0]
    block_scale = jnp.exp2(exps.astype(jnp.float32))
    grouped = codes.astype(jnp.float32).reshape(count, MODEL_WIDTH // QBLOCK, QBLOCK) * block_scale[:, :, None]
    return grouped.reshape(count, MODEL_WIDTH).astype(jnp.bfloat16)


def contract_trailing(left, right):
    return lax.dot_general(left, right, (((1,), (1,)), ((), ())), preferred_element_type=jnp.float32)


def contract_first(left, right):
    return lax.dot_general(left, right, (((0,), (0,)), ((), ())), preferred_element_type=jnp.float32)


def reference(attn, hidden, noisy, target, quantized_weight_codes, weight_exponents, adapter_down_map, adapter_up_transposed, gates, group_prompt, step_index):
    weight_matrix = dequantize(quantized_weight_codes, weight_exponents)
    level = noise_level(step_index)
    prompt_tok = jnp.repeat(group_prompt, TOK_DEV * N_SEQ)
    velocities = []
    gate_rows = []
    low_ranks = []
    for guidance_branch in range(2):
        gate_tok = gates[guidance_branch][prompt_tok]
        adapter_product = jnp.dot(attn[guidance_branch], adapter_down_map, preferred_element_type=jnp.float32).astype(jnp.bfloat16)
        projection_output = jnp.dot(attn[guidance_branch], weight_matrix, preferred_element_type=jnp.float32) + ADAPTER_STRENGTH * contract_trailing(adapter_product, adapter_up_transposed)
        velocities.append(hidden[guidance_branch].astype(jnp.float32) + gate_tok * projection_output)
        gate_rows.append(gate_tok)
        low_ranks.append(adapter_product)
    guided = velocities[1] + GUIDE * (velocities[0] - velocities[1])
    denoised = noisy.astype(jnp.float32) - level * guided
    reward_grad = REWARD * (target.astype(jnp.float32) - denoised)
    gradient_list = []
    down_total = jnp.zeros((MODEL_WIDTH, ADAPTER_RANK), jnp.float32)
    up_total = jnp.zeros((MODEL_WIDTH, ADAPTER_RANK), jnp.float32)
    for guidance_branch in range(2):
        branch_coef = GUIDE if guidance_branch == 0 else 1.0 - GUIDE
        gradient_before = (-level * branch_coef * gate_rows[guidance_branch] * reward_grad).astype(jnp.bfloat16)
        adapter_gradient = jnp.dot(gradient_before, adapter_up_transposed, preferred_element_type=jnp.float32).astype(jnp.bfloat16)
        gradient_list.append((contract_trailing(gradient_before, weight_matrix) + ADAPTER_STRENGTH * contract_trailing(adapter_gradient, adapter_down_map)).astype(jnp.bfloat16))
        down_total = down_total + ADAPTER_STRENGTH * contract_first(attn[guidance_branch], adapter_gradient)
        up_total = up_total + ADAPTER_STRENGTH * contract_first(gradient_before, low_ranks[guidance_branch])
    return jnp.stack(gradient_list), down_total, up_total
```

```python
import jax
import jax.numpy as jnp
from jax import lax
from jax.sharding import PartitionSpec as P

MODEL_WIDTH = 2432
QBLOCK = 128
RANK = 128
STEPS = 28
ZH, XN, YN = 4, 4, 8
PLANE = XN * YN
SLICE = MODEL_WIDTH // 4
ROWS = 19
TOK = 128

GUIDE = 4.5
REWARD = 0.08
ADAPTER_STRENGTH = 0.5
SHIFT = 3.0
F32 = jnp.float32
BF16 = jnp.bfloat16
EVERY = ("branch", "dp", "seq")


def swap(value, axis):
    return lax.ppermute(value, axis, [(0, 1), (1, 0)])


def noise_level(step_index):
    frac = step_index[0].astype(F32) / STEPS
    return SHIFT * frac / (1.0 + (SHIFT - 1.0) * frac)


def dequantize(codes, exps):
    count = codes.shape[0]
    block_scale = jnp.exp2(exps.astype(F32))
    grouped = (
        codes.astype(F32).reshape(count, MODEL_WIDTH // QBLOCK, QBLOCK)
        * block_scale[:, :, None]
    )
    return grouped.reshape(count, MODEL_WIDTH).astype(BF16)


def dot_nn(left, right):
    return lax.dot_general(left, right, (((1,), (0,)), ((), ())), preferred_element_type=F32)


def dot_nt(left, right):
    return lax.dot_general(left, right, (((1,), (1,)), ((), ())), preferred_element_type=F32)


def dot_tn(left, right):
    return lax.dot_general(left, right, (((0,), (0,)), ((), ())), preferred_element_type=F32)


def dp_index(z, x, y):
    return z * PLANE + x * YN + y


Y_GROUPS = [[dp_index(z, x, y) for y in range(YN)] for z in range(ZH) for x in range(XN)]
X_GROUPS = [[dp_index(z, x, y) for x in range(XN)] for z in range(ZH) for y in range(YN)]
XY_GROUPS = [[z * PLANE + i for i in range(PLANE)] for z in range(ZH)]


def along_z(value, by):
    pairs = [(d, (d + by * PLANE) % (ZH * PLANE)) for d in range(ZH * PLANE)]
    return lax.ppermute(value, "dp", pairs)


def place(branch, dp, seq):
    return (branch * ZH * PLANE + dp) * 2 + seq


def z_transposed(value, flip):
    pairs = []
    for z in range(ZH):
        for i in range(PLANE):
            for q in range(4):
                r = z ^ flip
                pairs.append((place(q // 2, z * PLANE + i, q % 2), place(r // 2, q * PLANE + i, r % 2)))
    return lax.ppermute(value, EVERY, pairs)


def gathered_weight(codes, exps, q, z):
    local = dequantize(codes, exps).reshape(ROWS, 4, SLICE)
    mine = lax.dynamic_index_in_dim(local, q, 1, keepdims=False)
    parts = [along_z(mine, 3), along_z(mine, 2), along_z(mine, 1), mine]
    ring = jnp.stack(parts + parts[:3])
    ordered = lax.dynamic_slice_in_dim(ring, 3 - z, 4, 0)
    lined = lax.all_gather(ordered, "dp", axis=0, axis_index_groups=Y_GROUPS)
    square = lined.transpose(1, 0, 2, 3).reshape(SLICE, SLICE)
    whole = lax.all_gather(square, "dp", axis=0, axis_index_groups=X_GROUPS)
    return whole.reshape(MODEL_WIDTH, SLICE)


def per_device(
    attn,
    hidden,
    noisy,
    target,
    quantized_weight_codes,
    weight_exponents,
    adapter_down_map,
    adapter_up_transposed,
    gates,
    group_prompt,
    step_index,
):
    b = lax.axis_index("branch")
    s = lax.axis_index("seq")
    z = lax.axis_index("dp") // PLANE
    q = 2 * b + s
    weight = gathered_weight(quantized_weight_codes, weight_exponents, q, z)

    level = noise_level(step_index)
    own = attn[0].reshape(TOK, ZH, XN, YN * ROWS).transpose(0, 2, 1, 3).reshape(TOK, MODEL_WIDTH)
    from_seq = swap(own, "seq")
    from_branch = swap(own, "branch")
    from_both = swap(from_seq, "branch")
    rows = jnp.concatenate([own, from_seq, from_branch, from_both], 0)

    is_first = b == 0
    shared = jnp.where(is_first, noisy, target)
    outgoing = jnp.stack([hidden[0], shared]).reshape(2, TOK, 4, SLICE).transpose(2, 0, 1, 3)
    incoming = lax.all_to_all(outgoing, ("branch", "seq"), 0, 0)
    pick = lambda i, j: lax.dynamic_index_in_dim(incoming[:, j], i, 0, keepdims=False).astype(F32)
    hid = [pick(q ^ k, 0) for k in range(4)]
    lift = [pick(2 + t, 1) - pick(t, 1) for t in (s, 1 - s)]

    selector = (jnp.arange(gates.shape[1], dtype=jnp.int32) == group_prompt[0]).astype(F32)
    gate_row = jnp.sum(selector[:, None] * gates[0], axis=0)
    gate_other = swap(gate_row, "branch")
    cut = lambda v: lax.dynamic_slice_in_dim(v, q * SLICE, SLICE, 0)
    g_own, g_other = cut(gate_row), cut(gate_other)
    c_own = jnp.where(is_first, F32(GUIDE), F32(1.0 - GUIDE))
    c_other = jnp.where(is_first, F32(1.0 - GUIDE), F32(GUIDE))

    up_slice = cut(adapter_up_transposed)
    down_turned = (
        adapter_down_map.reshape(ZH, XN, YN * ROWS, RANK).transpose(1, 0, 2, 3).reshape(MODEL_WIDTH, RANK)
    )
    low_rank = dot_nn(rows, down_turned).astype(BF16)
    projected = dot_nn(rows, weight) + ADAPTER_STRENGTH * dot_nt(low_rank, up_slice)
    projected = projected.reshape(4, TOK, SLICE)
    gradients = []
    for t in range(2):
        v_own = hid[t] + g_own * projected[t]
        v_other = hid[2 + t] + g_other * projected[2 + t]
        guided = c_own * v_own + c_other * v_other
        reward_grad = REWARD * (lift[t] + level * guided)
        gradients.append((
            (-level * c_own * g_own * reward_grad).astype(BF16),
            (-level * c_other * g_other * reward_grad).astype(BF16),
        ))
    before = jnp.concatenate([gradients[0][0], gradients[1][0], gradients[0][1], gradients[1][1]], 0)

    low_part = dot_nn(before, up_slice)
    low_part16 = low_part.astype(BF16)
    pair = low_part + jnp.roll(swap(low_part16, "branch").astype(F32), 2 * TOK, axis=0)
    far = swap(pair.astype(BF16), "seq").astype(F32).reshape(2, 2, TOK, RANK)[:, ::-1].reshape(4 * TOK, RANK)
    low_grad = (pair + far).astype(BF16)
    columns = lax.dynamic_index_in_dim(rows.reshape(4 * TOK, XN, ZH, YN * ROWS), q, 2, keepdims=False)
    term_down = ADAPTER_STRENGTH * dot_tn(columns.reshape(4 * TOK, SLICE), low_grad)
    term_up = ADAPTER_STRENGTH * dot_tn(before, low_rank)
    terms = jnp.stack([term_down.astype(BF16), term_up.astype(BF16)]).reshape(2, PLANE, ROWS, RANK)
    terms = terms.transpose(1, 0, 2, 3).reshape(PLANE, 2 * ROWS, RANK)
    spread = lax.all_to_all(terms, "dp", 0, 0, axis_index_groups=XY_GROUPS)
    plane_sum = jnp.sum(spread.astype(F32), axis=0)
    got = [z_transposed(plane_sum, k) for k in range(4)]
    total = (got[0] + got[1]) + (got[2] + got[3])

    part = (
        dot_nt(before, weight) + ADAPTER_STRENGTH * dot_nt(low_part16, down_turned)
    ).reshape(4, TOK, MODEL_WIDTH)
    near_far = swap(part[3].astype(BF16), "branch").astype(F32)
    near = swap(part[2].astype(BF16), "branch").astype(F32)
    across = swap((part[1] + near_far).astype(BF16), "seq").astype(F32)
    grad = (part[0] + near + across).astype(BF16)
    grad = grad.reshape(TOK, XN, ZH, YN * ROWS).transpose(0, 2, 1, 3).reshape(TOK, MODEL_WIDTH)
    return (grad[None], total[:ROWS], total[ROWS:])


def solution(mesh):
    return jax.shard_map(
        per_device,
        mesh=mesh,
        in_specs=(
            P("branch", ("dp", "seq"), None),
            P("branch", ("dp", "seq"), None),
            P(("dp", "seq"), None),
            P(("dp", "seq"), None),
            P("dp", None),
            P("dp", None),
            P(),
            P(),
            P("branch", None, None),
            P("dp"),
            P(),
        ),
        out_specs=(P("branch", ("dp", "seq"), None), P("dp", None), P("dp", None)),
        check_vma=False,
    )
```

```python
import jax
import jax.numpy as jnp
from jax import lax
from jax.experimental import pallas as pl
from jax.experimental.pallas import tpu as pltpu
from jax.sharding import PartitionSpec as P

MODEL_WIDTH = 2432
QBLOCK = 128
RANK = 128
STEPS = 28
ZH, XN, YN = 4, 4, 8
PLANE = XN * YN
SLICE = MODEL_WIDTH // 4
ROWS = 19
TOK = 128

GUIDE = 4.5
REWARD = 0.08
ADAPTER_STRENGTH = 0.5
SHIFT = 3.0
F32 = jnp.float32
BF16 = jnp.bfloat16
EVERY = ("branch", "dp", "seq")


def swap(value, axis):
    return lax.ppermute(value, axis, [(0, 1), (1, 0)])


def noise_level(step_index):
    frac = step_index[0].astype(F32) / STEPS
    return SHIFT * frac / (1.0 + (SHIFT - 1.0) * frac)


def dequantize(codes, exps):
    count = codes.shape[0]
    block_scale = jnp.exp2(exps.astype(F32))
    grouped = (
        codes.astype(F32).reshape(count, MODEL_WIDTH // QBLOCK, QBLOCK)
        * block_scale[:, :, None]
    )
    return grouped.reshape(count, MODEL_WIDTH).astype(BF16)


def dot_nn(left, right):
    return lax.dot_general(left, right, (((1,), (0,)), ((), ())), preferred_element_type=F32)


def dot_nt(left, right):
    return lax.dot_general(left, right, (((1,), (1,)), ((), ())), preferred_element_type=F32)


def dot_tn(left, right):
    return lax.dot_general(left, right, (((0,), (0,)), ((), ())), preferred_element_type=F32)


def dp_index(z, x, y):
    return z * PLANE + x * YN + y


Z_GROUPS = [[dp_index(z, x, y) for z in range(ZH)] for x in range(XN) for y in range(YN)]
Y_GROUPS = [[dp_index(z, x, y) for y in range(YN)] for z in range(ZH) for x in range(XN)]
X_GROUPS = [[dp_index(z, x, y) for x in range(XN)] for z in range(ZH) for y in range(YN)]
XY_GROUPS = [[z * PLANE + i for i in range(PLANE)] for z in range(ZH)]


def to_all(value, groups):
    copies = jnp.broadcast_to(value, (len(groups[0]),) + value.shape)
    return lax.all_to_all(copies, "dp", 0, 0, axis_index_groups=groups)


def place(branch, dp, seq):
    return (branch * ZH * PLANE + dp) * 2 + seq


def z_transposed(value, flip):
    pairs = []
    for z in range(ZH):
        for i in range(PLANE):
            for q in range(4):
                r = z ^ flip
                pairs.append((place(q // 2, z * PLANE + i, q % 2), place(r // 2, q * PLANE + i, r % 2)))
    return lax.ppermute(value, EVERY, pairs)


def own_columns(codes, exps, q):
    local = dequantize(codes, exps).reshape(ROWS, 4, SLICE)
    return lax.dynamic_index_in_dim(local, q, 1, keepdims=False)


def lanes(refs):
    return jnp.concatenate([ref[...] for ref in refs], 1)


def call(kernel, outs, flops, *args, **more):
    return pl.pallas_call(
        kernel,
        out_shape=[jax.ShapeDtypeStruct(shape, kind) for shape, kind in outs],
        compiler_params=pltpu.CompilerParams(vmem_limit_bytes=24 * 2**20),
        cost_estimate=pl.CostEstimate(flops=flops, bytes_accessed=8 * 10**6, transcendentals=0),
        **more,
    )(*args)


def adapter_kernel(own, seq, branch, both, down, up, lift, lift_far, a_own, a_other, low_rank, base):
    rows = lanes((own, seq, branch, both))
    low = dot_tn(down[...], rows).astype(BF16)
    low_rank[...] = low
    adapted = ADAPTER_STRENGTH * dot_nn(up[...], low)
    base[...] = lanes((lift, lift_far)) - a_own[...] * adapted[:, :2 * TOK] - a_other[...] * adapted[:, 2 * TOK:]


def forward_kernel(own, seq, branch, both, weight, base, a_own, a_other, up, before, low, product):
    step = pl.program_id(0)
    part = dot_tn(weight[...], lanes((own, seq, branch, both)))

    @pl.when(step == 0)
    def _():
        product[...] = part

    @pl.when((step > 0) & (step < XN - 1))
    def _():
        product[...] += part

    @pl.when(step == XN - 1)
    def _():
        whole = product[...] + part
        first, second = a_own[...], a_other[...]
        reward_grad = REWARD * (base[...] - first * whole[:, :2 * TOK] - second * whole[:, 2 * TOK:])
        grad = jnp.concatenate([first * reward_grad, second * reward_grad], 1).astype(BF16)
        before[...] = grad
        low[...] = dot_tn(up[...], grad)


def backward_kernel(before, weight, low, down, home, cross, near, far):
    part = dot_nn(weight[...], before[...]) + ADAPTER_STRENGTH * dot_nn(down[...], low[...].astype(BF16))
    for block, out in enumerate((home, cross, near, far)):
        out[...] = part[:, block * TOK:(block + 1) * TOK].astype(out.dtype)


def fixed(*shape):
    return pl.BlockSpec(shape, lambda n: (0, 0))


def rows_of(width):
    return pl.BlockSpec((SLICE, width), lambda n: (n, 0))


def forward(tokens, weight, base, a_own, a_other, up):
    return call(
        forward_kernel,
        [((SLICE, 4 * TOK), BF16), ((RANK, 4 * TOK), F32)],
        2 * 512 * 2432 * 608,
        *tokens, weight, base, a_own, a_other, up,
        grid=(XN,),
        in_specs=[rows_of(TOK)] * 4 + [rows_of(SLICE), fixed(SLICE, 2 * TOK), fixed(SLICE, 1), fixed(SLICE, 1), fixed(SLICE, RANK)],
        out_specs=[fixed(SLICE, 4 * TOK), fixed(RANK, 4 * TOK)],
        scratch_shapes=[pltpu.VMEM((SLICE, 4 * TOK), F32)],
    )


def backward(before, weight, low, down):
    shape = (MODEL_WIDTH, TOK)
    return call(
        backward_kernel,
        [(shape, F32), (shape, F32), (shape, BF16), (shape, BF16)],
        2 * 512 * 2432 * 736,
        before, weight, low, down,
        grid=(XN,),
        in_specs=[fixed(SLICE, 4 * TOK), rows_of(SLICE), fixed(RANK, 4 * TOK), rows_of(RANK)],
        out_specs=[rows_of(TOK)] * 4,
    )


def per_device(
    attn,
    hidden,
    noisy,
    target,
    quantized_weight_codes,
    weight_exponents,
    adapter_down_map,
    adapter_up_transposed,
    gates,
    group_prompt,
    step_index,
):
    b = lax.axis_index("branch")
    s = lax.axis_index("seq")
    q = 2 * b + s
    level = noise_level(step_index)
    is_first = b == 0
    mine = own_columns(quantized_weight_codes, weight_exponents, q)
    plane = to_all(mine, Z_GROUPS).reshape(ZH * ROWS, SLICE)
    plane, hidden = lax.optimization_barrier((plane, hidden))
    lined = to_all(plane, Y_GROUPS)

    own = attn[0].T.reshape(ZH, XN, YN * ROWS, TOK).transpose(1, 0, 2, 3).reshape(MODEL_WIDTH, TOK)
    from_seq = swap(own, "seq")
    from_branch = swap(own, "branch")

    c_own = jnp.where(is_first, F32(GUIDE), F32(1.0 - GUIDE))
    c_other = jnp.where(is_first, F32(1.0 - GUIDE), F32(GUIDE))
    half = lambda v, i: lax.dynamic_slice_in_dim(v, i * 2 * SLICE, 2 * SLICE, 1).astype(F32)
    hid_other = swap(lax.dynamic_slice_in_dim(hidden[0], (1 - b) * 2 * SLICE, 2 * SLICE, 1), "branch").astype(F32)
    lift = half(target, b) - half(noisy, b) + level * (c_own * half(hidden[0], b) + c_other * hid_other)
    lift = jnp.stack([lift[:, :SLICE].T, lift[:, SLICE:].T])
    take = lambda i: lax.dynamic_index_in_dim(lift, i, 0, keepdims=False)
    lift_near = take(s)
    lift_far = swap(take(1 - s), "seq")

    lined, from_seq, from_branch = lax.optimization_barrier((lined, from_seq, from_branch))
    square = lined.reshape(YN, ZH, ROWS, SLICE).transpose(1, 0, 2, 3).reshape(SLICE, SLICE)
    weight = to_all(square, X_GROUPS).reshape(MODEL_WIDTH, SLICE)
    from_both = swap(from_seq, "branch")
    tokens = (own, from_seq, from_branch, from_both)

    selector = (jnp.arange(gates.shape[1], dtype=jnp.int32) == group_prompt[0]).astype(F32)
    gate_row = jnp.sum(selector[:, None] * gates[0], axis=0)
    gate_other = swap(gate_row, "branch")
    cut = lambda v: lax.dynamic_slice_in_dim(v, q * SLICE, SLICE, 0)
    a_own = (-level * c_own * cut(gate_row))[:, None]
    a_other = (-level * c_other * cut(gate_other))[:, None]
    up_slice = cut(adapter_up_transposed)
    down_turned = (
        adapter_down_map.reshape(ZH, XN, YN * ROWS, RANK).transpose(1, 0, 2, 3).reshape(MODEL_WIDTH, RANK)
    )
    low_rank, base = call(
        adapter_kernel,
        [((RANK, 4 * TOK), BF16), ((SLICE, 2 * TOK), F32)],
        2 * 512 * 128 * 3040,
        *tokens, down_turned, up_slice, lift_near, lift_far, a_own, a_other,
    )
    before, low_part = forward(tokens, weight, base, a_own, a_other, up_slice)

    blocks = lambda v, *which: jnp.concatenate([v[:, i * TOK:(i + 1) * TOK] for i in which], 1)
    from_core = swap(low_part.astype(BF16), "branch").astype(F32)
    pair = low_part + blocks(from_core, 2, 3, 0, 1)
    pair16 = pair.astype(BF16)
    pair16, before_late = lax.optimization_barrier((pair16, before))
    from_chip = swap(pair16, "seq").astype(F32)
    low_grad = (pair + blocks(from_chip, 1, 0, 3, 2)).astype(BF16)
    mine_of = lambda v: lax.dynamic_index_in_dim(v.reshape(XN, ZH, YN * ROWS, TOK), q, 1, keepdims=False)
    columns = jnp.concatenate([mine_of(v).reshape(SLICE, TOK) for v in tokens], 1)
    term_down = ADAPTER_STRENGTH * dot_nt(columns, low_grad)
    term_up = ADAPTER_STRENGTH * dot_nt(before_late, low_rank)
    terms = jnp.stack([term_down.astype(BF16), term_up.astype(BF16)]).reshape(2, PLANE, ROWS, RANK)
    terms = terms.transpose(1, 0, 2, 3).reshape(PLANE, 2 * ROWS, RANK)
    spread = lax.all_to_all(terms, "dp", 0, 0, axis_index_groups=XY_GROUPS)
    plane_sum = jnp.sum(spread.astype(F32), axis=0)
    got = [z_transposed(plane_sum, k) for k in range(4)]
    total = (got[0] + got[1]) + (got[2] + got[3])

    home, cross, near, far = backward(before_late, weight, low_part, down_turned)
    cross = (cross + swap(far, "branch").astype(F32)).astype(BF16)
    grad = (home + swap(near, "branch").astype(F32) + swap(cross, "seq").astype(F32)).astype(BF16)
    grad = grad.reshape(XN, ZH, YN * ROWS, TOK).transpose(1, 0, 2, 3).reshape(MODEL_WIDTH, TOK).T
    return (grad[None], total[:ROWS], total[ROWS:])


def solution(mesh):
    return jax.shard_map(
        per_device,
        mesh=mesh,
        in_specs=(
            P("branch", ("dp", "seq"), None),
            P("branch", ("dp", "seq"), None),
            P(("dp", "seq"), None),
            P(("dp", "seq"), None),
            P("dp", None),
            P("dp", None),
            P(),
            P(),
            P("branch", None, None),
            P("dp"),
            P(),
        ),
        out_specs=(P("branch", ("dp", "seq"), None), P("dp", None), P("dp", None)),
        check_vma=False,
    )
```

```python
import math

import jax
import jax.numpy as jnp
import numpy as np
from jax import lax
from jax.experimental import pallas as pl
from jax.experimental.pallas import tpu as pltpu
from jax.sharding import PartitionSpec as P

MODEL_WIDTH = 2432
QBLOCK = 128
RANK = 128
STEPS = 28
ZH, XN, YN = 4, 4, 8
PLANE = XN * YN
SLICE = MODEL_WIDTH // 4
ROWS = 19
PADDED = 24
TOK = 128

GUIDE = 4.5
REWARD = 0.08
ADAPTER_STRENGTH = 0.5
SHIFT = 3.0
F32 = jnp.float32
BF16 = jnp.bfloat16
EVERY = ("branch", "dp", "seq")


def swap(value, axis):
    return lax.ppermute(value, axis, [(0, 1), (1, 0)])


def noise_level(step_index):
    frac = step_index[0].astype(F32) / STEPS
    return SHIFT * frac / (1.0 + (SHIFT - 1.0) * frac)


def dequantize(codes, exps):
    count = codes.shape[0]
    block_scale = jnp.exp2(exps.astype(F32))
    grouped = (
        codes.astype(F32).reshape(count, MODEL_WIDTH // QBLOCK, QBLOCK)
        * block_scale[:, :, None]
    )
    return grouped.reshape(count, MODEL_WIDTH).astype(BF16)


def dot_nn(left, right):
    return lax.dot_general(left, right, (((1,), (0,)), ((), ())), preferred_element_type=F32)


def dot_nt(left, right):
    return lax.dot_general(left, right, (((1,), (1,)), ((), ())), preferred_element_type=F32)


def dot_tn(left, right):
    return lax.dot_general(left, right, (((0,), (0,)), ((), ())), preferred_element_type=F32)


def dp_index(z, x, y):
    return z * PLANE + x * YN + y


Z_GROUPS = [[dp_index(z, x, y) for z in range(ZH)] for x in range(XN) for y in range(YN)]
Y_GROUPS = [[dp_index(z, x, y) for y in range(YN)] for z in range(ZH) for x in range(XN)]
XY_GROUPS = [[z * PLANE + i for i in range(PLANE)] for z in range(ZH)]


def to_all(value, groups):
    copies = jnp.broadcast_to(value, (len(groups[0]),) + value.shape)
    return lax.all_to_all(copies, "dp", 0, 0, axis_index_groups=groups)


def along_x(value, by):
    pairs = []
    for z in range(ZH):
        for x in range(XN):
            for y in range(YN):
                pairs.append((dp_index(z, x, y), dp_index(z, (x + by) % XN, y)))
    return lax.ppermute(value, "dp", pairs)


def place(branch, dp, seq):
    return (branch * ZH * PLANE + dp) * 2 + seq


def z_transposed(value, flip):
    pairs = []
    for z in range(ZH):
        for i in range(PLANE):
            for q in range(4):
                r = z ^ flip
                pairs.append((place(q // 2, z * PLANE + i, q % 2), place(r // 2, q * PLANE + i, r % 2)))
    return lax.ppermute(value, EVERY, pairs)


def own_columns(codes, exps, q):
    local = dequantize(codes, exps).reshape(ROWS, 4, SLICE)
    return lax.dynamic_index_in_dim(local, q, 1, keepdims=False)


SPREAD = np.zeros((PLANE * PADDED, SLICE), np.float32)
for _i in range(PLANE):
    for _j in range(ROWS):
        SPREAD[PADDED * _i + _j, ROWS * _i + _j] = 1.0


def x_block(ref, x):
    return ref[:, x].astype(F32).reshape(SLICE, ref.shape[-1]).astype(BF16)


def call(kernel, outs, flops, *args, places=None, **more):
    specs = [pl.BlockSpec(memory_space=pltpu.VMEM)] * len(args)
    if places is not None:
        args, specs = (places,) + args, [pl.BlockSpec(memory_space=pltpu.SMEM)] + specs
    more = more or dict(in_specs=specs)
    moved = sum(a.size * a.dtype.itemsize for a in args)
    moved += sum(math.prod(shape) * jnp.dtype(kind).itemsize for shape, kind in outs)
    return pl.pallas_call(
        kernel,
        out_shape=[jax.ShapeDtypeStruct(shape, kind) for shape, kind in outs],
        compiler_params=pltpu.CompilerParams(vmem_limit_bytes=24 * 2**20),
        cost_estimate=pl.CostEstimate(flops=flops, bytes_accessed=moved, transcendentals=0),
        **more,
    )(*args)


def features(places, own, other, down, rows, low_rank):
    low = jnp.zeros((2 * TOK, RANK), F32)
    for c in range(XN):
        part = jnp.concatenate([x_block(ref, places[c]).T for ref in (own, other)], 0)
        rows[c] = part
        low = low + dot_nn(part, x_block(down, places[c]))
    low_rank[...] = low.astype(BF16)


def far_kernel(places, own, other, down, near_rank, up, lift, far_lift, a_own, a_other, rows, low_rank, base, far_base):
    features(places, own, other, down, rows, low_rank)
    for rank, source, out in ((near_rank, lift, base), (low_rank, far_lift, far_base)):
        adapted = ADAPTER_STRENGTH * dot_nt(rank[...], up[...])
        out[...] = source[...] - a_own[...] * adapted[:TOK] - a_other[...] * adapted[TOK:]


def piece(upper, lower):
    return jnp.concatenate([upper[...], lower[...]], 0)


def near_kernel(rows, far_rows, *refs):
    weights, product = refs[:-1], refs[-1]
    for i, ref in enumerate((rows, far_rows)):
        total = dot_nn(ref[0], piece(*weights[:2]))
        for c in range(1, XN - 1):
            total = total + dot_nn(ref[c], piece(*weights[2 * c:2 * c + 2]))
        product[2 * TOK * i:2 * TOK * (i + 1)] = total


def forward_kernel(product, rows, far_rows, upper, lower, base, far_base, a_own, a_other, up, before, low):
    weight = piece(upper, lower)
    first, second = a_own[...], a_other[...]
    for i, (ref, lift) in enumerate(((rows, base), (far_rows, far_base))):
        part = slice(2 * TOK * i, 2 * TOK * (i + 1))
        whole = product[part] + dot_nn(ref[XN - 1], weight)
        reward_grad = REWARD * (lift[...] - first * whole[:TOK] - second * whole[TOK:])
        grad = jnp.concatenate([first * reward_grad, second * reward_grad], 0).astype(BF16)
        before[part] = grad
        low[part] = dot_nn(grad, up[...])


def backward_kernel(places, before, low, down, *refs):
    weights, (keep, send) = refs[:-2], refs[-2:]
    before_t = before[...].T
    low_t = low[...].astype(BF16).T
    for c in range(XN):
        part = dot_nn(piece(*weights[2 * c:2 * c + 2]), before_t)
        part = part + ADAPTER_STRENGTH * dot_nn(x_block(down, places[c]), low_t)
        for out, start in ((keep, 0), (send, TOK)):
            both = jnp.concatenate([part[:, start:start + TOK], part[:, start + 2 * TOK:start + 3 * TOK]], 1)
            out[:, places[c]] = both.reshape(ZH, YN * ROWS, 2 * TOK).astype(BF16)


def join_kernel(keep, got, home, cross):
    both = keep[...].astype(F32) + got[...].astype(F32)
    home[...] = both[..., :TOK]
    cross[...] = both[..., TOK:].astype(BF16)


def finish_kernel(home, across, grad):
    grad[...] = (home[...].reshape(MODEL_WIDTH, TOK) + across[...].astype(F32).reshape(MODEL_WIDTH, TOK)).T.astype(BF16)


def terms_kernel(quarter, pair, far, up, spread, *refs):
    tokens, terms = refs[:-1], refs[-1]
    far = far[...].astype(F32)
    low = (pair[...] + jnp.concatenate([far[2 * TOK:], far[:2 * TOK]], 0)).astype(BF16)
    columns = jnp.concatenate([ref[0] for ref in tokens], 1)
    down = (ADAPTER_STRENGTH * dot_nn(columns, low)).astype(BF16)
    both = dot_nn(spread[...], jnp.concatenate([down, up[...]], 1))
    first = both[:, :RANK].reshape(PLANE, PADDED, RANK)
    second = pltpu.roll(both[:, RANK:], ROWS - 16, 0).reshape(PLANE, PADDED, RANK)
    middle = first[:, 16:] + second[:, :8]
    terms[...] = jnp.concatenate([first[:, :16], middle, second[:, 8:]], 1).astype(BF16)


def by_x(value):
    return value.reshape(ZH, XN, YN * ROWS, value.shape[-1])


def terms_of(q, pair, far, up, tokens):
    whole = lambda *shape: pl.BlockSpec(shape, lambda n, quarter: (0,) * len(shape))
    return pl.pallas_call(
        terms_kernel,
        out_shape=jax.ShapeDtypeStruct((PLANE, 40, RANK), BF16),
        grid_spec=pltpu.PrefetchScalarGridSpec(
            num_scalar_prefetch=1,
            grid=(1,),
            in_specs=[whole(4 * TOK, RANK), whole(4 * TOK, RANK), whole(SLICE, RANK), whole(PLANE * PADDED, SLICE)]
            + [pl.BlockSpec((1, SLICE, TOK), lambda n, quarter: (quarter[0], 0, 0))] * 4,
            out_specs=whole(PLANE, 40, RANK),
        ),
        compiler_params=pltpu.CompilerParams(vmem_limit_bytes=24 * 2**20),
        cost_estimate=pl.CostEstimate(flops=2 * 512 * 768 * 128, bytes_accessed=3 * 10**6, transcendentals=0),
    )(q.astype(jnp.int32)[None], pair, far, up, jnp.asarray(SPREAD, BF16), *tokens)


def backward(places, before, low, down, weights):
    shape = (ZH, XN, YN * ROWS, 2 * TOK)
    return call(
        backward_kernel, [(shape, BF16), (shape, BF16)], 2 * 512 * 2432 * 736,
        before, low, by_x(down), *weights, places=places,
    )


def per_device(
    attn,
    hidden,
    noisy,
    target,
    quantized_weight_codes,
    weight_exponents,
    adapter_down_map,
    adapter_up_transposed,
    gates,
    group_prompt,
    step_index,
):
    b = lax.axis_index("branch")
    s = lax.axis_index("seq")
    q = 2 * b + s
    level = noise_level(step_index)
    is_first = b == 0
    mine = own_columns(quantized_weight_codes, weight_exponents, q)
    plane = to_all(mine, Z_GROUPS).reshape(ZH * ROWS, SLICE)
    plane, hidden = lax.optimization_barrier((plane, hidden))
    lined = to_all(plane, Y_GROUPS)

    own = attn[0].T
    from_seq = swap(own, "seq")
    from_branch = swap(own, "branch")
    x = (lax.axis_index("dp") // YN) % XN
    places = jnp.stack([(x + k) % XN for k in (0, XN - 1, 1, 2)]).astype(jnp.int32)
    ranks = [((XN, 2 * TOK, SLICE), BF16), ((2 * TOK, RANK), BF16)]
    rows, low_rank = call(features, ranks, 0, by_x(own), by_x(from_branch), by_x(adapter_down_map), places=places)

    selector = (jnp.arange(gates.shape[1], dtype=jnp.int32) == group_prompt[0]).astype(F32)
    gate_row = jnp.sum(selector[:, None] * gates[0], axis=0)
    gate_other = swap(gate_row, "branch")
    hid_other = swap(lax.dynamic_slice_in_dim(hidden[0], (1 - b) * 2 * SLICE, 2 * SLICE, 1), "branch")
    lined, from_seq, rows, low_rank, gate_other, hid_other = lax.optimization_barrier(
        (lined, from_seq, rows, low_rank, gate_other, hid_other)
    )

    square = lined.reshape(YN, ZH, ROWS, SLICE).transpose(1, 0, 2, 3).reshape(SLICE, SLICE)
    square = lax.optimization_barrier(square)
    here = [square[:SLICE // 2], square[SLICE // 2:]]
    here[0], here[1], from_seq, hid_other = lax.optimization_barrier((here[0], here[1], from_seq, hid_other))
    left = [along_x(here[0], 1), along_x(here[1], 1)]
    right = [along_x(here[0], -1), along_x(here[1], -1)]

    c_own = jnp.where(is_first, F32(GUIDE), F32(1.0 - GUIDE))
    c_other = jnp.where(is_first, F32(1.0 - GUIDE), F32(GUIDE))
    half = lambda v, i: lax.dynamic_slice_in_dim(v, i * 2 * SLICE, 2 * SLICE, 1).astype(F32)
    lift = half(target, b) - half(noisy, b) + level * (c_own * half(hidden[0], b) + c_other * hid_other.astype(F32))
    lift = jnp.stack([lift[:, :SLICE], lift[:, SLICE:]])
    take = lambda i: lax.dynamic_index_in_dim(lift, i, 0, keepdims=False)
    lift_near = take(s)
    lift_far = take(1 - s)

    cut = lambda v: lax.dynamic_slice_in_dim(v, q * SLICE, SLICE, 0)
    a_own = (-level * c_own * cut(gate_row))[None]
    a_other = (-level * c_other * cut(gate_other))[None]
    up_slice = cut(adapter_up_transposed)
    lift_far = swap(lift_far, "seq")
    from_both = swap(from_seq, "branch")
    opposite = [along_x(left[0], 1), along_x(right[1], -1)]
    near_weights = here + left + right
    far_rows, far_low_rank, base, far_base = call(
        far_kernel,
        ranks + [((TOK, SLICE), F32)] * 2,
        2 * 256 * 128 * 3600,
        by_x(from_seq), by_x(from_both), by_x(adapter_down_map), low_rank, up_slice, lift_near, lift_far, a_own, a_other,
        places=places,
    )
    product = call(
        near_kernel, [((4 * TOK, SLICE), F32)], 2 * 512 * 1824 * 608, rows, far_rows, *near_weights,
    )[0]
    before, low_part = call(
        forward_kernel,
        [((4 * TOK, SLICE), BF16), ((4 * TOK, RANK), F32)],
        2 * 512 * 608 * 736,
        product, rows, far_rows, *opposite, base, far_base, a_own, a_other, up_slice,
    )

    blocks = lambda v, *which: jnp.concatenate([v[i * TOK:(i + 1) * TOK] for i in which], 0)
    from_core = swap(low_part.astype(BF16), "branch").astype(F32)
    pair = low_part + blocks(from_core, 1, 0, 3, 2)
    from_chip = swap(pair.astype(BF16), "seq")
    term_up = (ADAPTER_STRENGTH * dot_tn(before, jnp.concatenate([low_rank, far_low_rank], 0))).astype(BF16)
    tokens = [v.reshape(ZH, SLICE, TOK) for v in (own, from_branch, from_seq, from_both)]
    terms = terms_of(q, pair, from_chip, term_up, tokens)
    keep, send = backward(places, before, low_part, adapter_down_map, near_weights + opposite)
    terms, send, keep = lax.optimization_barrier((terms, send, keep))
    spread = lax.all_to_all(terms, "dp", 0, 0, axis_index_groups=XY_GROUPS)
    plane_sum = jnp.sum(spread.astype(F32), axis=0)
    total = z_transposed(plane_sum, 0) + z_transposed(plane_sum, 1)
    total = total + swap(total, "branch")

    shape = (ZH, XN, YN * ROWS, TOK)
    home, cross = call(join_kernel, [(shape, F32), (shape, BF16)], 2 * 2432 * 256, keep, swap(send, "branch"))
    grad = call(finish_kernel, [((TOK, MODEL_WIDTH), BF16)], 2432 * 128, home, swap(cross, "seq"))[0]
    return (grad[None], total[:ROWS], total[ROWS:2 * ROWS])


def solution(mesh):
    return jax.shard_map(
        per_device,
        mesh=mesh,
        in_specs=(
            P("branch", ("dp", "seq"), None),
            P("branch", ("dp", "seq"), None),
            P(("dp", "seq"), None),
            P(("dp", "seq"), None),
            P("dp", None),
            P("dp", None),
            P(),
            P(),
            P("branch", None, None),
            P("dp"),
            P(),
        ),
        out_specs=(P("branch", ("dp", "seq"), None), P("dp", None), P("dp", None)),
        check_vma=False,
    )
```

```python
import math

import jax
import jax.numpy as jnp
import numpy as np
from jax import lax
from jax.experimental import pallas as pl
from jax.experimental.pallas import tpu as pltpu
from jax.sharding import PartitionSpec as P

MODEL_WIDTH = 2432
QBLOCK = 128
RANK = 128
STEPS = 28
ZH, XN, YN = 4, 4, 8
PLANE = XN * YN
SLICE = MODEL_WIDTH // 4
ROWS = 19
PADDED = 24
TOK = 128

GUIDE = 4.5
REWARD = 0.08
ADAPTER_STRENGTH = 0.5
SHIFT = 3.0
F32 = jnp.float32
BF16 = jnp.bfloat16
EVERY = ("branch", "dp", "seq")


def swap(value, axis):
    return lax.ppermute(value, axis, [(0, 1), (1, 0)])


def noise_level(step_index):
    frac = step_index[0].astype(F32) / STEPS
    return SHIFT * frac / (1.0 + (SHIFT - 1.0) * frac)


def dequantize(codes, exps):
    count = codes.shape[0]
    block_scale = jnp.exp2(exps.astype(F32))
    grouped = (
        codes.astype(F32).reshape(count, MODEL_WIDTH // QBLOCK, QBLOCK)
        * block_scale[:, :, None]
    )
    return grouped.reshape(count, MODEL_WIDTH).astype(BF16)


def dot_nn(left, right):
    return lax.dot_general(left, right, (((1,), (0,)), ((), ())), preferred_element_type=F32)


def dot_nt(left, right):
    return lax.dot_general(left, right, (((1,), (1,)), ((), ())), preferred_element_type=F32)


def dot_tn(left, right):
    return lax.dot_general(left, right, (((0,), (0,)), ((), ())), preferred_element_type=F32)


def dp_index(z, x, y):
    return z * PLANE + x * YN + y


Z_GROUPS = [[dp_index(z, x, y) for z in range(ZH)] for x in range(XN) for y in range(YN)]
Y_GROUPS = [[dp_index(z, x, y) for y in range(YN)] for z in range(ZH) for x in range(XN)]
XY_GROUPS = [[z * PLANE + i for i in range(PLANE)] for z in range(ZH)]


def to_all(value, groups):
    copies = jnp.broadcast_to(value, (len(groups[0]),) + value.shape)
    return lax.all_to_all(copies, "dp", 0, 0, axis_index_groups=groups)


def along_x(value, by):
    pairs = []
    for z in range(ZH):
        for x in range(XN):
            for y in range(YN):
                pairs.append((dp_index(z, x, y), dp_index(z, (x + by) % XN, y)))
    return lax.ppermute(value, "dp", pairs)


def place(branch, dp, seq):
    return (branch * ZH * PLANE + dp) * 2 + seq


def z_transposed(value, flip):
    pairs = []
    for z in range(ZH):
        for i in range(PLANE):
            for q in range(4):
                r = z ^ flip
                pairs.append((place(q // 2, z * PLANE + i, q % 2), place(r // 2, q * PLANE + i, r % 2)))
    return lax.ppermute(value, EVERY, pairs)


def own_columns(codes, exps, q):
    local = dequantize(codes, exps).reshape(ROWS, 4, SLICE)
    return lax.dynamic_index_in_dim(local, q, 1, keepdims=False)


def lanes(refs):
    return jnp.concatenate([ref[...] for ref in refs], 1)


SPREAD = np.zeros((PLANE * PADDED, SLICE), np.float32)
for _i in range(PLANE):
    for _j in range(ROWS):
        SPREAD[PADDED * _i + _j, ROWS * _i + _j] = 1.0


def x_block(ref, x):
    return ref[:, x].astype(F32).reshape(SLICE, ref.shape[-1]).astype(BF16)


def call(kernel, outs, flops, *args, places=None, scratch=()):
    specs = [pl.BlockSpec(memory_space=pltpu.VMEM)] * len(args)
    if places is not None:
        args, specs = (places,) + args, [pl.BlockSpec(memory_space=pltpu.SMEM)] + specs
    moved = sum(a.size * a.dtype.itemsize for a in args)
    moved += sum(math.prod(shape) * jnp.dtype(kind).itemsize for shape, kind in outs)
    return pl.pallas_call(
        kernel,
        out_shape=[jax.ShapeDtypeStruct(shape, kind) for shape, kind in outs],
        compiler_params=pltpu.CompilerParams(vmem_limit_bytes=24 * 2**20),
        cost_estimate=pl.CostEstimate(flops=flops, bytes_accessed=moved, transcendentals=0),
        in_specs=specs,
        scratch_shapes=scratch,
    )(*args)


def features(slots, own, other, down, rows, low_rank, columns):
    low = jnp.zeros((2 * TOK, RANK), F32)
    for x in range(XN):
        for z in range(ZH):
            start = z * SLICE + x * YN * ROWS
            for i, ref in enumerate((own, other)):
                part = ref[:, start:start + YN * ROWS]
                rows[slots[x], i * TOK:(i + 1) * TOK, z * YN * ROWS:(z + 1) * YN * ROWS] = part
        low = low + dot_nn(rows[slots[x]], x_block(down, x))
    low_rank[...] = low.astype(BF16)
    for k in range(ZH):
        @pl.when(slots[XN] == k)
        def _():
            both = jnp.concatenate([ref[:, k * SLICE:(k + 1) * SLICE] for ref in (own, other)], 0)
            columns[...] = both.T


def arrange_kernel(lined, upper, lower, whole):
    for y in range(YN):
        block = lined[y].astype(F32)
        for z in range(ZH):
            start = (z * YN + y) * ROWS
            whole[start:start + ROWS] = block[z * ROWS:(z + 1) * ROWS]
    upper[...] = whole[:SLICE // 2].astype(BF16)
    lower[...] = whole[SLICE // 2:].astype(BF16)


def piece(upper, lower):
    return jnp.concatenate([upper[...], lower[...]], 0)


def near_kernel(rows, far_rows, *refs):
    weights, product = refs[:-1], refs[-1]
    for i, ref in enumerate((rows, far_rows)):
        total = dot_nn(ref[0], piece(*weights[:2]))
        for c in range(1, XN - 1):
            total = total + dot_nn(ref[c], piece(*weights[2 * c:2 * c + 2]))
        product[2 * TOK * i:2 * TOK * (i + 1)] = total


def forward_kernel(
    product, rows, far_rows, upper, lower, rank, far_rank, lift, far_lift, a_own, a_other, up, before, low
):
    weight = piece(upper, lower)
    first, second = a_own[...], a_other[...]
    for i, (ref, ranks, lifts) in enumerate(((rows, rank, lift), (far_rows, far_rank, far_lift))):
        part = slice(2 * TOK * i, 2 * TOK * (i + 1))
        whole = product[part] + dot_nn(ref[XN - 1], weight) + ADAPTER_STRENGTH * dot_nt(ranks[...], up[...])
        reward_grad = REWARD * (lifts[...] - first * whole[:TOK] - second * whole[TOK:])
        grad = jnp.concatenate([first * reward_grad, second * reward_grad], 0).astype(BF16)
        before[part] = grad
        low[part] = dot_nn(grad, up[...])


def backward_kernel(places, before, low, down, *refs):
    weights, (keep, send) = refs[:-2], refs[-2:]
    before_t = before[...].T
    low_t = low[...].astype(BF16).T
    for c in range(XN):
        part = dot_nn(piece(*weights[2 * c:2 * c + 2]), before_t)
        part = part + ADAPTER_STRENGTH * dot_nn(x_block(down, places[c]), low_t)
        for out, start in ((keep, 0), (send, TOK)):
            both = jnp.concatenate([part[:, start:start + TOK], part[:, start + 2 * TOK:start + 3 * TOK]], 1)
            out[:, places[c]] = both.reshape(ZH, YN * ROWS, 2 * TOK).astype(BF16)


def join_kernel(keep, got, home, cross):
    both = keep[...].astype(F32) + got[...].astype(F32)
    home[...] = both[..., :TOK]
    cross[...] = both[..., TOK:].astype(BF16)


def finish_kernel(home, across, grad):
    grad[...] = (home[...].reshape(MODEL_WIDTH, TOK) + across[...].astype(F32).reshape(MODEL_WIDTH, TOK)).T.astype(BF16)


def terms_kernel(pair, far, up, spread, columns, far_columns, terms):
    far = far[...].astype(F32)
    low = (pair[...] + jnp.concatenate([far[2 * TOK:], far[:2 * TOK]], 0)).astype(BF16)
    down = (ADAPTER_STRENGTH * dot_nn(lanes((columns, far_columns)), low)).astype(BF16)
    both = dot_nn(spread[...], jnp.concatenate([down, up[...]], 1))
    first = both[:, :RANK].reshape(PLANE, PADDED, RANK)
    second = pltpu.roll(both[:, RANK:], ROWS - 16, 0).reshape(PLANE, PADDED, RANK)
    middle = first[:, 16:] + second[:, :8]
    terms[...] = jnp.concatenate([first[:, :16], middle, second[:, 8:]], 1).astype(BF16)


def by_x(value):
    return value.reshape(ZH, XN, YN * ROWS, value.shape[-1])


def backward(places, before, low, down, weights):
    shape = (ZH, XN, YN * ROWS, 2 * TOK)
    return call(
        backward_kernel, [(shape, BF16), (shape, BF16)], 2 * 512 * 2432 * 736,
        before, low, by_x(down), *weights, places=places,
    )


def per_device(
    attn,
    hidden,
    noisy,
    target,
    quantized_weight_codes,
    weight_exponents,
    adapter_down_map,
    adapter_up_transposed,
    gates,
    group_prompt,
    step_index,
):
    b = lax.axis_index("branch")
    s = lax.axis_index("seq")
    q = 2 * b + s
    level = noise_level(step_index)
    is_first = b == 0
    mine = own_columns(quantized_weight_codes, weight_exponents, q)
    plane = to_all(mine, Z_GROUPS).reshape(ZH * ROWS, SLICE)
    plane, hidden = lax.optimization_barrier((plane, hidden))
    lined = to_all(plane, Y_GROUPS)

    own = attn[0]
    from_seq = swap(own, "seq")
    from_branch = swap(own, "branch")
    x = (lax.axis_index("dp") // YN) % XN
    places = jnp.stack([(x + k) % XN for k in (0, XN - 1, 1, 2)]).astype(jnp.int32)
    slots = jnp.array([0, 2, 3, 1], jnp.int32)[(jnp.arange(XN) - x) % XN]
    slots = jnp.concatenate([slots, q.astype(jnp.int32)[None]])
    kinds = [((XN, 2 * TOK, SLICE), BF16), ((2 * TOK, RANK), BF16), ((SLICE, 2 * TOK), BF16)]
    rows, low_rank, columns = call(features, kinds, 0, own, from_branch, by_x(adapter_down_map), places=slots)

    selector = (jnp.arange(gates.shape[1], dtype=jnp.int32) == group_prompt[0]).astype(F32)
    gate_row = jnp.sum(selector[:, None] * gates[0], axis=0)
    gate_other = swap(gate_row, "branch")
    half = lambda v, i: lax.dynamic_slice_in_dim(v, i * 2 * SLICE, 2 * SLICE, 1)
    hid_other = swap(half(hidden[0], 1 - b), "branch")

    here = call(
        arrange_kernel, [((SLICE // 2, SLICE), BF16)] * 2, 0, lined, scratch=[pltpu.VMEM((SLICE, SLICE), F32)],
    )
    *here, from_seq, rows, low_rank, columns, gate_other, hid_other = lax.optimization_barrier(
        (*here, from_seq, rows, low_rank, columns, gate_other, hid_other)
    )
    left = [along_x(here[0], 1), along_x(here[1], 1)]
    right = [along_x(here[0], -1), along_x(here[1], -1)]

    c_own = jnp.where(is_first, F32(GUIDE), F32(1.0 - GUIDE))
    c_other = jnp.where(is_first, F32(1.0 - GUIDE), F32(GUIDE))
    lift = half(target, b).astype(F32) - half(noisy, b).astype(F32)
    lift = lift + level * (c_own * half(hidden[0], b).astype(F32) + c_other * hid_other.astype(F32))
    lift = jnp.stack([lift[:, :SLICE], lift[:, SLICE:]])
    take = lambda i: lax.dynamic_index_in_dim(lift, i, 0, keepdims=False)
    lift_near = take(s)
    lift_far = take(1 - s)
    cut = lambda v: lax.dynamic_slice_in_dim(v, q * SLICE, SLICE, 0)
    a_own = (-level * c_own * cut(gate_row))[None]
    a_other = (-level * c_other * cut(gate_other))[None]
    up_slice = cut(adapter_up_transposed)
    lift_far = swap(lift_far, "seq")
    from_both = swap(from_seq, "branch")
    opposite = [along_x(left[0], 1), along_x(right[1], -1)]
    near_weights = here + left + right
    far_rows, far_low_rank, far_columns = call(
        features, kinds, 2 * 256 * 128 * 2432, from_seq, from_both, by_x(adapter_down_map), places=slots,
    )
    product = call(
        near_kernel, [((4 * TOK, SLICE), F32)], 2 * 512 * 1824 * 608, rows, far_rows, *near_weights,
    )[0]
    before, low_part = call(
        forward_kernel,
        [((4 * TOK, SLICE), BF16), ((4 * TOK, RANK), F32)],
        2 * 512 * 608 * 736,
        product, rows, far_rows, *opposite, low_rank, far_low_rank, lift_near, lift_far, a_own, a_other, up_slice,
    )

    blocks = lambda v, *which: jnp.concatenate([v[i * TOK:(i + 1) * TOK] for i in which], 0)
    from_core = swap(low_part.astype(BF16), "branch").astype(F32)
    pair = low_part + blocks(from_core, 1, 0, 3, 2)
    from_chip = swap(pair.astype(BF16), "seq")
    term_up = (ADAPTER_STRENGTH * dot_tn(before, jnp.concatenate([low_rank, far_low_rank], 0))).astype(BF16)
    terms = call(
        terms_kernel, [((PLANE, 40, RANK), BF16)], 2 * 512 * 768 * 128,
        pair, from_chip, term_up, jnp.asarray(SPREAD, BF16), columns, far_columns,
    )[0]
    keep, send = backward(places, before, low_part, adapter_down_map, near_weights + opposite)
    terms, send, keep = lax.optimization_barrier((terms, send, keep))
    spread = lax.all_to_all(terms, "dp", 0, 0, axis_index_groups=XY_GROUPS)
    plane_sum = jnp.sum(spread.astype(F32), axis=0)
    total = z_transposed(plane_sum, 0) + z_transposed(plane_sum, 1)

    shape = (ZH, XN, YN * ROWS, TOK)
    home, cross = call(join_kernel, [(shape, F32), (shape, BF16)], 2 * 2432 * 256, keep, swap(send, "branch"))
    grad = call(finish_kernel, [((TOK, MODEL_WIDTH), BF16)], 2432 * 128, home, swap(cross, "seq"))[0]
    total, grad = lax.optimization_barrier((total, grad))
    total = total + swap(total, "branch")
    return (grad[None], total[:ROWS], total[ROWS:2 * ROWS])


def solution(mesh):
    return jax.shard_map(
        per_device,
        mesh=mesh,
        in_specs=(
            P("branch", ("dp", "seq"), None),
            P("branch", ("dp", "seq"), None),
            P(("dp", "seq"), None),
            P(("dp", "seq"), None),
            P("dp", None),
            P("dp", None),
            P(),
            P(),
            P("branch", None, None),
            P("dp"),
            P(),
        ),
        out_specs=(P("branch", ("dp", "seq"), None), P("dp", None), P("dp", None)),
        check_vma=False,
    )
```

```python
import math

import jax
import jax.numpy as jnp
import numpy as np
from jax import lax
from jax.experimental import pallas as pl
from jax.experimental.pallas import tpu as pltpu
from jax.sharding import PartitionSpec as P

MODEL_WIDTH = 2432
QBLOCK = 128
RANK = 128
STEPS = 28
ZH, XN, YN = 4, 4, 8
PLANE = XN * YN
SLICE = MODEL_WIDTH // 4
ROWS = 19
PADDED = 24
TOK = 128

GUIDE = 4.5
REWARD = 0.08
ADAPTER_STRENGTH = 0.5
SHIFT = 3.0
F32 = jnp.float32
BF16 = jnp.bfloat16
EVERY = ("branch", "dp", "seq")


def swap(value, axis):
    return lax.ppermute(value, axis, [(0, 1), (1, 0)])


def noise_level(step_index):
    frac = step_index[0].astype(F32) / STEPS
    return SHIFT * frac / (1.0 + (SHIFT - 1.0) * frac)


def dequantize(codes, exps):
    count = codes.shape[0]
    block_scale = jnp.exp2(exps.astype(F32))
    grouped = (
        codes.astype(F32).reshape(count, MODEL_WIDTH // QBLOCK, QBLOCK)
        * block_scale[:, :, None]
    )
    return grouped.reshape(count, MODEL_WIDTH).astype(BF16)


def dot_nn(left, right):
    return lax.dot_general(left, right, (((1,), (0,)), ((), ())), preferred_element_type=F32)


def dot_nt(left, right):
    return lax.dot_general(left, right, (((1,), (1,)), ((), ())), preferred_element_type=F32)


def dot_tn(left, right):
    return lax.dot_general(left, right, (((0,), (0,)), ((), ())), preferred_element_type=F32)


def dp_index(z, x, y):
    return z * PLANE + x * YN + y


Z_GROUPS = [[dp_index(z, x, y) for z in range(ZH)] for x in range(XN) for y in range(YN)]
Y_GROUPS = [[dp_index(z, x, y) for y in range(YN)] for z in range(ZH) for x in range(XN)]
XY_GROUPS = [[z * PLANE + i for i in range(PLANE)] for z in range(ZH)]


def to_all(value, groups):
    copies = jnp.broadcast_to(value, (len(groups[0]),) + value.shape)
    return lax.all_to_all(copies, "dp", 0, 0, axis_index_groups=groups)


def along_x(value, by):
    pairs = []
    for z in range(ZH):
        for x in range(XN):
            for y in range(YN):
                pairs.append((dp_index(z, x, y), dp_index(z, (x + by) % XN, y)))
    return lax.ppermute(value, "dp", pairs)


def place(branch, dp, seq):
    return (branch * ZH * PLANE + dp) * 2 + seq


def z_transposed(value, flip):
    pairs = []
    for z in range(ZH):
        for i in range(PLANE):
            for q in range(4):
                r = z ^ flip
                pairs.append((place(q // 2, z * PLANE + i, q % 2), place(r // 2, q * PLANE + i, r % 2)))
    return lax.ppermute(value, EVERY, pairs)


def own_columns(codes, exps, q):
    local = dequantize(codes, exps).reshape(ROWS, 4, SLICE)
    return lax.dynamic_index_in_dim(local, q, 1, keepdims=False)


def lanes(refs):
    return jnp.concatenate([ref[...] for ref in refs], 1)


SPREAD = np.zeros((PLANE * PADDED, SLICE), np.float32)
for _i in range(PLANE):
    for _j in range(ROWS):
        SPREAD[PADDED * _i + _j, ROWS * _i + _j] = 1.0


def x_block(ref, x):
    return ref[:, x].astype(F32).reshape(SLICE, ref.shape[-1]).astype(BF16)


def call(kernel, outs, flops, *args, places=None, scratch=()):
    specs = [pl.BlockSpec(memory_space=pltpu.VMEM)] * len(args)
    if places is not None:
        args, specs = (places,) + args, [pl.BlockSpec(memory_space=pltpu.SMEM)] + specs
    moved = sum(a.size * a.dtype.itemsize for a in args)
    moved += sum(math.prod(shape) * jnp.dtype(kind).itemsize for shape, kind in outs)
    return pl.pallas_call(
        kernel,
        out_shape=[jax.ShapeDtypeStruct(shape, kind) for shape, kind in outs],
        compiler_params=pltpu.CompilerParams(vmem_limit_bytes=24 * 2**20),
        cost_estimate=pl.CostEstimate(flops=flops, bytes_accessed=moved, transcendentals=0),
        in_specs=specs,
        scratch_shapes=scratch,
    )(*args)


def features(slots, own, other, down, rows, low_rank, columns):
    low = jnp.zeros((2 * TOK, RANK), F32)
    for x in range(XN):
        for z in range(ZH):
            start = z * SLICE + x * YN * ROWS
            for i, ref in enumerate((own, other)):
                part = ref[:, start:start + YN * ROWS]
                rows[slots[x], i * TOK:(i + 1) * TOK, z * YN * ROWS:(z + 1) * YN * ROWS] = part
        low = low + dot_nn(rows[slots[x]], x_block(down, x))
    low_rank[...] = low.astype(BF16)
    for k in range(ZH):
        @pl.when(slots[XN] == k)
        def _():
            both = jnp.concatenate([ref[:, k * SLICE:(k + 1) * SLICE] for ref in (own, other)], 0)
            columns[...] = both.T


def arrange_kernel(lined, upper, lower, whole):
    for y in range(YN):
        block = lined[y].astype(F32)
        for z in range(ZH):
            start = (z * YN + y) * ROWS
            whole[start:start + ROWS] = block[z * ROWS:(z + 1) * ROWS]
    upper[...] = whole[:SLICE // 2].astype(BF16)
    lower[...] = whole[SLICE // 2:].astype(BF16)


def piece(upper, lower):
    return jnp.concatenate([upper[...], lower[...]], 0)


def near_kernel(rows, far_rows, *refs):
    weights, product = refs[:-1], refs[-1]
    for i, ref in enumerate((rows, far_rows)):
        total = dot_nn(ref[0], piece(*weights[:2]))
        for c in range(1, XN - 1):
            total = total + dot_nn(ref[c], piece(*weights[2 * c:2 * c + 2]))
        product[2 * TOK * i:2 * TOK * (i + 1)] = total


def forward_kernel(
    product, rows, far_rows, upper, lower, rank, far_rank, lift, far_lift, a_own, a_other, up, before, low
):
    weight = piece(upper, lower)
    first, second = a_own[...], a_other[...]
    for i, (ref, ranks, lifts) in enumerate(((rows, rank, lift), (far_rows, far_rank, far_lift))):
        part = slice(2 * TOK * i, 2 * TOK * (i + 1))
        whole = product[part] + dot_nn(ref[XN - 1], weight) + ADAPTER_STRENGTH * dot_nt(ranks[...], up[...])
        reward_grad = REWARD * (lifts[...].astype(F32) - first * whole[:TOK] - second * whole[TOK:])
        grad = jnp.concatenate([first * reward_grad, second * reward_grad], 0).astype(BF16)
        before[part] = grad
        low[part] = dot_nn(grad, up[...])


def backward_kernel(places, before, low, down, *refs):
    weights, (keep, send) = refs[:-2], refs[-2:]
    before_t = before[...].T
    low_t = low[...].astype(BF16).T
    for c in range(XN):
        part = dot_nn(piece(*weights[2 * c:2 * c + 2]), before_t)
        part = part + ADAPTER_STRENGTH * dot_nn(x_block(down, places[c]), low_t)
        for out, start in ((keep, 0), (send, TOK)):
            both = jnp.concatenate([part[:, start:start + TOK], part[:, start + 2 * TOK:start + 3 * TOK]], 1)
            out[:, places[c]] = both.reshape(ZH, YN * ROWS, 2 * TOK).astype(BF16)


def join_kernel(keep, got, home, cross):
    both = keep[...].astype(F32) + got[...].astype(F32)
    home[...] = both[..., :TOK]
    cross[...] = both[..., TOK:].astype(BF16)


def finish_kernel(home, across, grad):
    grad[...] = (home[...].reshape(MODEL_WIDTH, TOK) + across[...].astype(F32).reshape(MODEL_WIDTH, TOK)).T.astype(BF16)


def terms_kernel(pair, far, up, spread, columns, far_columns, terms):
    far = far[...].astype(F32)
    low = (pair[...] + jnp.concatenate([far[2 * TOK:], far[:2 * TOK]], 0)).astype(BF16)
    down = (ADAPTER_STRENGTH * dot_nn(lanes((columns, far_columns)), low)).astype(BF16)
    both = dot_nn(spread[...], jnp.concatenate([down, up[...]], 1))
    first = both[:, :RANK].reshape(PLANE, PADDED, RANK)
    second = pltpu.roll(both[:, RANK:], ROWS - 16, 0).reshape(PLANE, PADDED, RANK)
    middle = first[:, 16:] + second[:, :8]
    terms[...] = jnp.concatenate([first[:, :16], middle, second[:, 8:]], 1).astype(BF16)


def by_x(value):
    return value.reshape(ZH, XN, YN * ROWS, value.shape[-1])


def backward(places, before, low, down, weights):
    shape = (ZH, XN, YN * ROWS, 2 * TOK)
    return call(
        backward_kernel, [(shape, BF16), (shape, BF16)], 2 * 512 * 2432 * 736,
        before, low, by_x(down), *weights, places=places,
    )


def per_device(
    attn,
    hidden,
    noisy,
    target,
    quantized_weight_codes,
    weight_exponents,
    adapter_down_map,
    adapter_up_transposed,
    gates,
    group_prompt,
    step_index,
):
    b = lax.axis_index("branch")
    s = lax.axis_index("seq")
    q = 2 * b + s
    level = noise_level(step_index)
    is_first = b == 0
    mine = own_columns(quantized_weight_codes, weight_exponents, q)
    plane = to_all(mine, Z_GROUPS).reshape(ZH * ROWS, SLICE)
    plane, hidden = lax.optimization_barrier((plane, hidden))
    lined = to_all(plane, Y_GROUPS)

    own = attn[0]
    from_seq = swap(own, "seq")
    from_branch = swap(own, "branch")
    x = (lax.axis_index("dp") // YN) % XN
    places = jnp.stack([(x + k) % XN for k in (0, XN - 1, 1, 2)]).astype(jnp.int32)
    slots = jnp.array([0, 2, 3, 1], jnp.int32)[(jnp.arange(XN) - x) % XN]
    slots = jnp.concatenate([slots, q.astype(jnp.int32)[None]])
    kinds = [((XN, 2 * TOK, SLICE), BF16), ((2 * TOK, RANK), BF16), ((SLICE, 2 * TOK), BF16)]
    rows, low_rank, columns = call(features, kinds, 2 * 256 * 128 * 2432, own, from_branch, by_x(adapter_down_map), places=slots)

    selector = (jnp.arange(gates.shape[1], dtype=jnp.int32) == group_prompt[0]).astype(F32)
    gate_row = jnp.sum(selector[:, None] * gates[0], axis=0)
    gate_other = swap(gate_row, "branch")
    half = lambda v, i: lax.dynamic_slice_in_dim(v, i * 2 * SLICE, 2 * SLICE, 1)
    hid_other = swap(half(hidden[0], 1 - b), "branch")

    here = call(
        arrange_kernel, [((SLICE // 2, SLICE), BF16)] * 2, 1, lined, scratch=[pltpu.VMEM((SLICE, SLICE), F32)],
    )
    *here, from_seq, rows, low_rank, columns, gate_other, hid_other = lax.optimization_barrier(
        (*here, from_seq, rows, low_rank, columns, gate_other, hid_other)
    )
    left = [along_x(here[0], 1), along_x(here[1], 1)]
    right = [along_x(here[0], -1), along_x(here[1], -1)]

    c_own = jnp.where(is_first, F32(GUIDE), F32(1.0 - GUIDE))
    c_other = jnp.where(is_first, F32(1.0 - GUIDE), F32(GUIDE))
    lift = half(target, b).astype(F32) - half(noisy, b).astype(F32)
    lift = lift + level * (c_own * half(hidden[0], b).astype(F32) + c_other * hid_other.astype(F32))
    lift = jnp.stack([lift[:, :SLICE], lift[:, SLICE:]])
    take = lambda i: lax.dynamic_index_in_dim(lift, i, 0, keepdims=False)
    lift_near = take(s)
    lift_far = take(1 - s)
    cut = lambda v: lax.dynamic_slice_in_dim(v, q * SLICE, SLICE, 0)
    a_own = (-level * c_own * cut(gate_row))[None]
    a_other = (-level * c_other * cut(gate_other))[None]
    up_slice = cut(adapter_up_transposed)
    lift_far = swap(lift_far.astype(BF16), "seq")
    from_both = swap(from_seq, "branch")
    opposite = [along_x(left[0], 1), along_x(right[1], -1)]
    near_weights = here + left + right
    far_rows, far_low_rank, far_columns = call(
        features, kinds, 2 * 256 * 128 * 2432, from_seq, from_both, by_x(adapter_down_map), places=slots,
    )
    product = call(
        near_kernel, [((4 * TOK, SLICE), F32)], 2 * 512 * 1824 * 608, rows, far_rows, *near_weights,
    )[0]
    before, low_part = call(
        forward_kernel,
        [((4 * TOK, SLICE), BF16), ((4 * TOK, RANK), F32)],
        2 * 512 * 608 * 736,
        product, rows, far_rows, *opposite, low_rank, far_low_rank, lift_near, lift_far, a_own, a_other, up_slice,
    )

    blocks = lambda v, *which: jnp.concatenate([v[i * TOK:(i + 1) * TOK] for i in which], 0)
    from_core = swap(low_part.astype(BF16), "branch").astype(F32)
    pair = low_part + blocks(from_core, 1, 0, 3, 2)
    from_chip = swap(pair.astype(BF16), "seq")
    term_up = (ADAPTER_STRENGTH * dot_tn(before, jnp.concatenate([low_rank, far_low_rank], 0))).astype(BF16)
    terms = call(
        terms_kernel, [((PLANE, 40, RANK), BF16)], 2 * 512 * 768 * 128,
        pair, from_chip, term_up, jnp.asarray(SPREAD, BF16), columns, far_columns,
    )[0]
    keep, send = backward(places, before, low_part, adapter_down_map, near_weights + opposite)
    terms, send, keep = lax.optimization_barrier((terms, send, keep))
    spread = lax.all_to_all(terms, "dp", 0, 0, axis_index_groups=XY_GROUPS)
    plane_sum = jnp.sum(spread.astype(F32), axis=0)
    total = z_transposed(plane_sum, 0) + z_transposed(plane_sum, 1)

    shape = (ZH, XN, YN * ROWS, TOK)
    home, cross = call(join_kernel, [(shape, F32), (shape, BF16)], 2 * 2432 * 256, keep, swap(send, "branch"))
    across = swap(cross, "seq")
    total, across = lax.optimization_barrier((total, across))
    total = total + swap(total, "branch")
    grad = call(finish_kernel, [((TOK, MODEL_WIDTH), BF16)], 2432 * 128, home, across)[0]
    return (grad[None], total[:ROWS], total[ROWS:2 * ROWS])


def solution(mesh):
    return jax.shard_map(
        per_device,
        mesh=mesh,
        in_specs=(
            P("branch", ("dp", "seq"), None),
            P("branch", ("dp", "seq"), None),
            P(("dp", "seq"), None),
            P(("dp", "seq"), None),
            P("dp", None),
            P("dp", None),
            P(),
            P(),
            P("branch", None, None),
            P("dp"),
            P(),
        ),
        out_specs=(P("branch", ("dp", "seq"), None), P("dp", None), P("dp", None)),
        check_vma=False,
    )
```

```python
import math

import jax
import jax.numpy as jnp
import numpy as np
from jax import lax
from jax.experimental import pallas as pl
from jax.experimental.pallas import tpu as pltpu
from jax.sharding import PartitionSpec as P

MODEL_WIDTH = 2432
QBLOCK = 128
RANK = 128
STEPS = 28
ZH, XN, YN = 4, 4, 8
PLANE = XN * YN
SLICE = MODEL_WIDTH // 4
ROWS = 19
PADDED = 24
TOK = 128

GUIDE = 4.5
REWARD = 0.08
ADAPTER_STRENGTH = 0.5
SHIFT = 3.0
F32 = jnp.float32
BF16 = jnp.bfloat16
EVERY = ("branch", "dp", "seq")


def swap(value, axis):
    return lax.ppermute(value, axis, [(0, 1), (1, 0)])


def noise_level(step_index):
    frac = step_index[0].astype(F32) / STEPS
    return SHIFT * frac / (1.0 + (SHIFT - 1.0) * frac)


def dequantize(codes, exps):
    count = codes.shape[0]
    block_scale = jnp.exp2(exps.astype(F32))
    grouped = (
        codes.astype(F32).reshape(count, MODEL_WIDTH // QBLOCK, QBLOCK)
        * block_scale[:, :, None]
    )
    return grouped.reshape(count, MODEL_WIDTH).astype(BF16)


def dot_nn(left, right):
    return lax.dot_general(left, right, (((1,), (0,)), ((), ())), preferred_element_type=F32)


def dot_nt(left, right):
    return lax.dot_general(left, right, (((1,), (1,)), ((), ())), preferred_element_type=F32)


def dot_tn(left, right):
    return lax.dot_general(left, right, (((0,), (0,)), ((), ())), preferred_element_type=F32)


def dp_index(z, x, y):
    return z * PLANE + x * YN + y


Z_GROUPS = [[dp_index(z, x, y) for z in range(ZH)] for x in range(XN) for y in range(YN)]
Y_GROUPS = [[dp_index(z, x, y) for y in range(YN)] for z in range(ZH) for x in range(XN)]
XY_GROUPS = [[z * PLANE + i for i in range(PLANE)] for z in range(ZH)]


def to_all(value, groups):
    copies = jnp.broadcast_to(value, (len(groups[0]),) + value.shape)
    return lax.all_to_all(copies, "dp", 0, 0, axis_index_groups=groups)


def along_x(value, by):
    pairs = []
    for z in range(ZH):
        for x in range(XN):
            for y in range(YN):
                pairs.append((dp_index(z, x, y), dp_index(z, (x + by) % XN, y)))
    return lax.ppermute(value, "dp", pairs)


def place(branch, dp, seq):
    return (branch * ZH * PLANE + dp) * 2 + seq


def z_transposed(value, flip):
    pairs = []
    for z in range(ZH):
        for i in range(PLANE):
            for q in range(4):
                r = z ^ flip
                pairs.append((place(q // 2, z * PLANE + i, q % 2), place(r // 2, q * PLANE + i, r % 2)))
    return lax.ppermute(value, EVERY, pairs)


def own_columns(codes, exps, q):
    local = dequantize(codes, exps).reshape(ROWS, 4, SLICE)
    return lax.dynamic_index_in_dim(local, q, 1, keepdims=False)


def lanes(refs):
    return jnp.concatenate([ref[...] for ref in refs], 1)


SPREAD = np.zeros((PLANE * PADDED, SLICE), np.float32)
for _i in range(PLANE):
    for _j in range(ROWS):
        SPREAD[PADDED * _i + _j, ROWS * _i + _j] = 1.0


def x_block(ref, x):
    return ref[:, x].astype(F32).reshape(SLICE, ref.shape[-1]).astype(BF16)


def call(kernel, outs, flops, *args, places=None, scratch=(), space=pltpu.VMEM):
    specs = [pl.BlockSpec(memory_space=space)] * len(args)
    if places is not None:
        args, specs = (places,) + args, [pl.BlockSpec(memory_space=pltpu.SMEM)] + specs
    moved = sum(a.size * a.dtype.itemsize for a in args)
    moved += sum(math.prod(shape) * jnp.dtype(kind).itemsize for shape, kind in outs)
    return pl.pallas_call(
        kernel,
        out_shape=[jax.ShapeDtypeStruct(shape, kind) for shape, kind in outs],
        compiler_params=pltpu.CompilerParams(vmem_limit_bytes=24 * 2**20),
        cost_estimate=pl.CostEstimate(flops=flops, bytes_accessed=moved, transcendentals=0),
        in_specs=specs,
        scratch_shapes=scratch,
    )(*args)


def features(slots, own, other, down, rows, low_rank, columns):
    low = jnp.zeros((2 * TOK, RANK), F32)
    for x in range(XN):
        for z in range(ZH):
            start = z * SLICE + x * YN * ROWS
            for i, ref in enumerate((own, other)):
                part = ref[:, start:start + YN * ROWS]
                rows[slots[x], i * TOK:(i + 1) * TOK, z * YN * ROWS:(z + 1) * YN * ROWS] = part
        low = low + dot_nn(rows[slots[x]], x_block(down, x))
    low_rank[...] = low.astype(BF16)
    for k in range(ZH):
        @pl.when(slots[XN] == k)
        def _():
            both = jnp.concatenate([ref[:, k * SLICE:(k + 1) * SLICE] for ref in (own, other)], 0)
            columns[...] = both.T


def arrange_kernel(lined, upper, lower, whole):
    for y in range(YN):
        block = lined[y].astype(F32)
        for z in range(ZH):
            start = (z * YN + y) * ROWS
            whole[start:start + ROWS] = block[z * ROWS:(z + 1) * ROWS]
    upper[...] = whole[:SLICE // 2].astype(BF16)
    lower[...] = whole[SLICE // 2:].astype(BF16)


def piece(upper, lower):
    return jnp.concatenate([upper[...], lower[...]], 0)


def near_kernel(rows, far_rows, *refs):
    weights, product = refs[:-1], refs[-1]
    for i, ref in enumerate((rows, far_rows)):
        total = dot_nn(ref[0], piece(*weights[:2]))
        for c in range(1, XN - 1):
            total = total + dot_nn(ref[c], piece(*weights[2 * c:2 * c + 2]))
        product[2 * TOK * i:2 * TOK * (i + 1)] = total


def forward_kernel(
    product, rows, far_rows, upper, lower, rank, far_rank, lift, far_lift, a_own, a_other, up, before, low
):
    weight = piece(upper, lower)
    first, second = a_own[...], a_other[...]
    for i, (ref, ranks, lifts) in enumerate(((rows, rank, lift), (far_rows, far_rank, far_lift))):
        part = slice(2 * TOK * i, 2 * TOK * (i + 1))
        whole = product[part] + dot_nn(ref[XN - 1], weight) + ADAPTER_STRENGTH * dot_nt(ranks[...], up[...])
        reward_grad = REWARD * (lifts[...].astype(F32) - first * whole[:TOK] - second * whole[TOK:])
        grad = jnp.concatenate([first * reward_grad, second * reward_grad], 0).astype(BF16)
        before[part] = grad
        low[part] = dot_nn(grad, up[...])


def backward_kernel(places, before, low, down, *refs):
    weights, (keep, send) = refs[:-2], refs[-2:]
    before_t = before[...].T
    low_t = low[...].astype(BF16).T
    for c in range(XN):
        part = dot_nn(piece(*weights[2 * c:2 * c + 2]), before_t)
        part = part + ADAPTER_STRENGTH * dot_nn(x_block(down, places[c]), low_t)
        for out, start in ((keep, 0), (send, TOK)):
            both = jnp.concatenate([part[:, start:start + TOK], part[:, start + 2 * TOK:start + 3 * TOK]], 1)
            out[:, places[c]] = both.reshape(ZH, YN * ROWS, 2 * TOK).astype(BF16)


def join_kernel(keep, got, home, cross, kept, gotten, arrived):
    copies = [
        pltpu.make_async_copy(source, target, arrived.at[i])
        for i, (source, target) in enumerate(((keep, kept), (got, gotten)))
    ]
    for copy in copies:
        copy.start()
    for copy in copies:
        copy.wait()
    both = kept[...].astype(F32) + gotten[...].astype(F32)
    home[...] = both[:, :TOK]
    cross[...] = both[:, TOK:].astype(BF16)


def join(keep, got):
    shape, wide = (MODEL_WIDTH, TOK), (MODEL_WIDTH, 2 * TOK)
    return call(
        join_kernel, [(shape, F32), (shape, BF16)], 2 * 2432 * 256, keep.reshape(wide), got.reshape(wide),
        scratch=[pltpu.VMEM(wide, BF16), pltpu.VMEM(wide, BF16), pltpu.SemaphoreType.DMA((2,))],
        space=pl.ANY,
    )


def finish_kernel(home, across, grad):
    grad[...] = (home[...] + across[...].astype(F32)).T.astype(BF16)


def terms_kernel(pair, far, up, spread, columns, far_columns, terms):
    far = far[...].astype(F32)
    low = (pair[...] + jnp.concatenate([far[2 * TOK:], far[:2 * TOK]], 0)).astype(BF16)
    down = (ADAPTER_STRENGTH * dot_nn(lanes((columns, far_columns)), low)).astype(BF16)
    both = dot_nn(spread[...], jnp.concatenate([down, up[...]], 1))
    first = both[:, :RANK].reshape(PLANE, PADDED, RANK)
    second = pltpu.roll(both[:, RANK:], ROWS - 16, 0).reshape(PLANE, PADDED, RANK)
    middle = first[:, 16:] + second[:, :8]
    terms[...] = jnp.concatenate([first[:, :16], middle, second[:, 8:]], 1).astype(BF16)


def by_x(value):
    return value.reshape(ZH, XN, YN * ROWS, value.shape[-1])


def backward(places, before, low, down, weights):
    shape = (ZH, XN, YN * ROWS, 2 * TOK)
    return call(
        backward_kernel, [(shape, BF16), (shape, BF16)], 2 * 512 * 2432 * 736,
        before, low, by_x(down), *weights, places=places,
    )


def per_device(
    attn,
    hidden,
    noisy,
    target,
    quantized_weight_codes,
    weight_exponents,
    adapter_down_map,
    adapter_up_transposed,
    gates,
    group_prompt,
    step_index,
):
    b = lax.axis_index("branch")
    s = lax.axis_index("seq")
    q = 2 * b + s
    level = noise_level(step_index)
    is_first = b == 0
    mine = own_columns(quantized_weight_codes, weight_exponents, q)
    plane = to_all(mine, Z_GROUPS).reshape(ZH * ROWS, SLICE)
    plane, hidden = lax.optimization_barrier((plane, hidden))
    lined = to_all(plane, Y_GROUPS)

    own = attn[0]
    from_seq = swap(own, "seq")
    from_branch = swap(own, "branch")
    x = (lax.axis_index("dp") // YN) % XN
    places = jnp.stack([(x + k) % XN for k in (0, XN - 1, 1, 2)]).astype(jnp.int32)
    slots = jnp.array([0, 2, 3, 1], jnp.int32)[(jnp.arange(XN) - x) % XN]
    slots = jnp.concatenate([slots, q.astype(jnp.int32)[None]])
    kinds = [((XN, 2 * TOK, SLICE), BF16), ((2 * TOK, RANK), BF16), ((SLICE, 2 * TOK), BF16)]
    rows, low_rank, columns = call(features, kinds, 2 * 256 * 128 * 2432, own, from_branch, by_x(adapter_down_map), places=slots)

    selector = (jnp.arange(gates.shape[1], dtype=jnp.int32) == group_prompt[0]).astype(F32)
    gate_row = jnp.sum(selector[:, None] * gates[0], axis=0)
    gate_other = swap(gate_row, "branch")
    half = lambda v, i: lax.dynamic_slice_in_dim(v, i * 2 * SLICE, 2 * SLICE, 1)
    hid_other = swap(half(hidden[0], 1 - b), "branch")

    here = call(
        arrange_kernel, [((SLICE // 2, SLICE), BF16)] * 2, 1, lined, scratch=[pltpu.VMEM((SLICE, SLICE), F32)],
    )
    *here, from_seq, rows, low_rank, columns, gate_other, hid_other = lax.optimization_barrier(
        (*here, from_seq, rows, low_rank, columns, gate_other, hid_other)
    )
    left = [along_x(here[0], 1), along_x(here[1], 1)]
    right = [along_x(here[0], -1), along_x(here[1], -1)]

    c_own = jnp.where(is_first, F32(GUIDE), F32(1.0 - GUIDE))
    c_other = jnp.where(is_first, F32(1.0 - GUIDE), F32(GUIDE))
    lift = half(target, b).astype(F32) - half(noisy, b).astype(F32)
    lift = lift + level * (c_own * half(hidden[0], b).astype(F32) + c_other * hid_other.astype(F32))
    lift = jnp.stack([lift[:, :SLICE], lift[:, SLICE:]])
    take = lambda i: lax.dynamic_index_in_dim(lift, i, 0, keepdims=False)
    lift_near = take(s)
    lift_far = take(1 - s)
    cut = lambda v: lax.dynamic_slice_in_dim(v, q * SLICE, SLICE, 0)
    a_own = (-level * c_own * cut(gate_row))[None]
    a_other = (-level * c_other * cut(gate_other))[None]
    up_slice = cut(adapter_up_transposed)
    lift_far = swap(lift_far.astype(BF16), "seq")
    from_both = swap(from_seq, "branch")
    opposite = [along_x(left[0], 1), along_x(right[1], -1)]
    near_weights = here + left + right
    far_rows, far_low_rank, far_columns = call(
        features, kinds, 2 * 256 * 128 * 2432, from_seq, from_both, by_x(adapter_down_map), places=slots,
    )
    product = call(
        near_kernel, [((4 * TOK, SLICE), F32)], 2 * 512 * 1824 * 608, rows, far_rows, *near_weights,
    )[0]
    before, low_part = call(
        forward_kernel,
        [((4 * TOK, SLICE), BF16), ((4 * TOK, RANK), F32)],
        2 * 512 * 608 * 736,
        product, rows, far_rows, *opposite, low_rank, far_low_rank, lift_near, lift_far, a_own, a_other, up_slice,
    )

    blocks = lambda v, *which: jnp.concatenate([v[i * TOK:(i + 1) * TOK] for i in which], 0)
    from_core = swap(low_part.astype(BF16), "branch").astype(F32)
    pair = low_part + blocks(from_core, 1, 0, 3, 2)
    from_chip = swap(pair.astype(BF16), "seq")
    term_up = (ADAPTER_STRENGTH * dot_tn(before, jnp.concatenate([low_rank, far_low_rank], 0))).astype(BF16)
    terms = call(
        terms_kernel, [((PLANE, 40, RANK), BF16)], 2 * 512 * 768 * 128,
        pair, from_chip, term_up, jnp.asarray(SPREAD, BF16), columns, far_columns,
    )[0]
    keep, send = backward(places, before, low_part, adapter_down_map, near_weights + opposite)
    terms, send, keep = lax.optimization_barrier((terms, send, keep))
    spread = lax.all_to_all(terms, "dp", 0, 0, axis_index_groups=XY_GROUPS)
    plane_sum = jnp.sum(spread.astype(F32), axis=0)
    total = z_transposed(plane_sum, 0) + z_transposed(plane_sum, 1)

    home, cross = join(keep, swap(send, "branch"))
    across = swap(cross, "seq")
    total, across = lax.optimization_barrier((total, across))
    total = total + swap(total, "branch")
    grad = call(finish_kernel, [((TOK, MODEL_WIDTH), BF16)], 2432 * 128, home, across)[0]
    return (grad[None], total[:ROWS], total[ROWS:2 * ROWS])


def solution(mesh):
    return jax.shard_map(
        per_device,
        mesh=mesh,
        in_specs=(
            P("branch", ("dp", "seq"), None),
            P("branch", ("dp", "seq"), None),
            P(("dp", "seq"), None),
            P(("dp", "seq"), None),
            P("dp", None),
            P("dp", None),
            P(),
            P(),
            P("branch", None, None),
            P("dp"),
            P(),
        ),
        out_specs=(P("branch", ("dp", "seq"), None), P("dp", None), P("dp", None)),
        check_vma=False,
    )
```
